512 devices in a mesh: section: 32 (over y, z_lo), tensor: 16 (over z_hi, x, core).
Axes of the slice: x: 4, y: 4, z: 16 (z_hi: 2, z_lo: 8; z = z_hi * 8 + z_lo), core: 2. Of those that a mesh axis runs over, the one named last changes fastest.
Arguments:
- inputs: bfloat16 [4, 64, 8192], P(None, 'section', 'tensor'), may hold values from -6 to 6
- cotangent: bfloat16 [4, 64, 8192], P(None, 'section', 'tensor'), may hold values from -1.5 to 1.5
- plan: int32 [4], replicated, may hold values from 0 to 3, each once
- weights: bfloat16 [32, 1664, 8192], P('section', None, 'tensor'), may hold values from -0.0625 to 0.0625
Outputs:
- grads: bfloat16 [32, 1664, 8192], P('section', None, 'tensor')
The draws below stay inside these ranges and needn't reach their ends.
Inputs may be any that keep to these rules, and one draw needn't show every extreme that they name: `plan`: a permutation of the 4 micro-batches.
All inputs are finite; a program needn't handle non-finite values.
Results may differ from the reference program's by a relative error of at most 0.028.
Values may be sent and summed in bfloat16 or wider, within the bound.
No kernel may reach another device: no remote copies, remote signals or barrier semaphores. Data moves between devices by JAX's collectives and lax.ppermute only.
A program may use at most 64 MiB of HBM per device.

```python
import jax
import jax.numpy as jnp
from jax import lax

D = 8192
FS = 26624
MB = 4
ROWS = 64
COPIES = 16
PIECES = 32
FP = 1664
N_TENSOR = 16


def shard_levels(stream_key, extent, pieces, least, top_value):
    gain = 1.0
    for dim, parts in pieces:
        steps = jax.random.uniform(jax.random.fold_in(jax.random.fold_in(stream_key, 6), dim), (parts,), jnp.float32, least / len(pieces), top_value / len(pieces))
        gain = gain * jnp.repeat(jnp.exp(steps), extent[dim] // parts).reshape((-1,) + (1,) * (len(extent) - 1 - dim))
    return gain


def gaussian(stream_key, shape, width, limit, shards=(), kind=jnp.bfloat16):
    result = width * jax.random.normal(stream_key, shape, jnp.float32)
    if shards:
        result = result * shard_levels(stream_key, shape, shards, -0.22, 0.18)
    return jnp.clip(result, -limit, limit).astype(kind)


def setup_inputs(seed: int = 0) -> dict:
    key_list = jax.random.split(jax.random.key(seed), 5)
    return {
        "inputs": gaussian(key_list[0], (MB, ROWS, D), 1.0, 6.0, ((1, 32), (2, 16))),
        "cotangent": gaussian(key_list[1], (MB, ROWS, D), 0.1, 1.5, ((1, 32), (2, 16))),
        "plan": jax.random.permutation(key_list[2], MB).astype(jnp.int32),
        "weights": gaussian(key_list[3], (PIECES, FP, D), D ** -0.5, 0.0625, ((0, 32), (2, 16))),
    }


def grouped(values, weight):
    row_count = values.shape[0]
    group_width = D // N_TENSOR
    split_values = values.reshape(row_count, N_TENSOR, group_width).transpose(1, 0, 2)
    split_weight = weight.reshape(FS, N_TENSOR, group_width).transpose(1, 0, 2)

    def add_group(running, operands):
        partial_value = jnp.dot(operands[0], operands[1].T, preferred_element_type=jnp.float32)
        rounded = lax.optimization_barrier(partial_value.astype(jnp.bfloat16))
        return running + rounded.astype(jnp.float32), None

    running, unused = lax.scan(add_group, jnp.zeros((row_count, FS), jnp.float32), (split_values, split_weight))
    return running


def reference(inputs, cotangent, plan, weights):
    entering = jnp.take(inputs, plan, axis=0).reshape(MB * ROWS, D)
    returning = cotangent.reshape(MB * ROWS, D)
    gate_rows = weights[:COPIES].reshape(FS, D)
    down_rows = weights[COPIES:].reshape(FS, D)
    pre_sum = grouped(entering, gate_rows)
    hidden = jax.nn.silu(pre_sum).astype(jnp.bfloat16)
    grad_hidden = grouped(returning, down_rows).astype(jnp.bfloat16)
    logistic = jax.nn.sigmoid(pre_sum)
    slope = logistic * (1.0 + pre_sum * (1.0 - logistic))
    grad_pre = (grad_hidden.astype(jnp.float32) * slope).astype(jnp.bfloat16)
    grad_gate = jnp.dot(grad_pre.T, entering, preferred_element_type=jnp.float32).astype(jnp.bfloat16)
    grad_down = jnp.dot(hidden.T, returning, preferred_element_type=jnp.float32).astype(jnp.bfloat16)
    return jnp.concatenate([grad_gate, grad_down], axis=0).reshape(PIECES, FP, D)
```

```python
import jax
import jax.numpy as jnp
import numpy as np
from jax import lax
from jax.sharding import Mesh, PartitionSpec as P

SECTION = ("half", "yl", "zl")
TENSOR = ("zh", "x", "core")
OWNERS = ("half", "x", "core")


def local(inputs, cotangent, plan, weights):
    piece = weights[0]
    width = piece.shape[1]
    hidden_units = piece.shape[0]
    sections = lax.axis_size(SECTION)
    owners = lax.axis_size(OWNERS)

    entering = jnp.take(inputs, plan, axis=0).reshape(1, -1, width)
    returning = cotangent.reshape(1, -1, width)
    outgoing = jnp.concatenate(
        [
            jnp.broadcast_to(entering, (sections // 2,) + entering.shape[1:]),
            jnp.broadcast_to(returning, (sections // 2,) + returning.shape[1:]),
        ]
    )
    rows = lax.all_to_all(outgoing, SECTION, 0, 0).reshape(-1, width)
    row_count = rows.shape[0]

    partial = jnp.einsum("rd,fd->rf", rows, piece, preferred_element_type=jnp.float32)
    partial = partial.astype(jnp.bfloat16).reshape(owners, row_count // owners, hidden_units)
    gathered = lax.all_to_all(partial, OWNERS, 0, 0)
    gathered = gathered.reshape((2, owners // 2) + gathered.shape[1:])
    near = jnp.sum(gathered.astype(jnp.float32), axis=1).astype(jnp.bfloat16)
    far = lax.ppermute(near, "zh", [(0, 1), (1, 0)])
    total = near.astype(jnp.float32) + far.astype(jnp.float32)
    pre_sum = total[0]
    grad_hidden = total[1].astype(jnp.bfloat16).astype(jnp.float32)
    logistic = jax.nn.sigmoid(pre_sum)
    hidden = (pre_sum * logistic).astype(jnp.bfloat16)
    grad_pre = (grad_hidden * logistic * (1.0 + pre_sum * (1.0 - logistic))).astype(jnp.bfloat16)

    answer = jnp.concatenate(
        [
            jnp.broadcast_to(grad_pre[None], (owners // 2,) + grad_pre.shape),
            jnp.broadcast_to(hidden[None], (owners // 2,) + hidden.shape),
        ]
    )
    left = lax.all_to_all(answer, OWNERS, 0, 0).reshape(row_count, hidden_units)
    grads = jnp.einsum("rf,rd->fd", left, rows, preferred_element_type=jnp.float32)
    return grads.astype(jnp.bfloat16)[None]


def solution(mesh):
    fine = Mesh(
        np.asarray(mesh.devices).reshape(2, 2, 8, 2, 4, 2),
        ("half", "yl", "zl", "zh", "x", "core"),
    )
    placed = (
        P(None, SECTION, TENSOR),
        P(None, SECTION, TENSOR),
        P(),
        P(SECTION, None, TENSOR),
    )
    return jax.shard_map(
        local, mesh=fine, in_specs=placed, out_specs=P(SECTION, None, TENSOR), check_vma=False
    )
```

```python
import jax
import jax.numpy as jnp
import numpy as np
from jax import lax
from jax.experimental import pallas as pl
from jax.experimental.pallas import tpu as pltpu
from jax.sharding import Mesh, PartitionSpec as P

SECTION = ("half", "yl", "zl")
TENSOR = ("zh", "x", "core")
OWNERS = ("half", "x")


def pack_kernel(plan_ref, inputs_ref, cotangent_ref, out_ref):
    batches = inputs_ref.shape[0]
    half = out_ref.shape[0] // 2
    entering = jnp.concatenate(
        [inputs_ref[plan_ref[k]].astype(jnp.float32) for k in range(batches)], axis=0
    )
    returning = jnp.concatenate(
        [cotangent_ref[k].astype(jnp.float32) for k in range(batches)], axis=0
    )
    for first, rows in ((0, entering), (half, returning)):
        rows = rows.astype(out_ref.dtype)
        out_ref[pl.ds(first, half)] = jnp.broadcast_to(rows[None], (half,) + rows.shape)


def pack(plan, inputs, cotangent, sections):
    batches, tokens, width = inputs.shape
    return pl.pallas_call(
        pack_kernel,
        out_shape=jax.ShapeDtypeStruct((sections, batches * tokens, width), inputs.dtype),
        in_specs=[
            pl.BlockSpec(memory_space=pltpu.SMEM),
            pl.BlockSpec(memory_space=pltpu.VMEM),
            pl.BlockSpec(memory_space=pltpu.VMEM),
        ],
        out_specs=pl.BlockSpec(memory_space=pltpu.VMEM),
    )(plan, inputs, cotangent)


def local(inputs, cotangent, plan, weights):
    piece = weights[0]
    hidden_units, width = piece.shape
    sections = lax.axis_size(SECTION)
    owners = lax.axis_size(OWNERS)
    core = lax.axis_index("core")
    twin = [(0, 1), (1, 0)]

    rows = lax.all_to_all(pack(plan, inputs, cotangent, sections), SECTION, 0, 0)
    rows = rows.reshape(2, -1, width)
    half_rows = rows.shape[1]
    rows_here = lax.dynamic_index_in_dim(rows, core, 0, keepdims=False)
    rows_there = lax.dynamic_index_in_dim(rows, 1 - core, 0, keepdims=False)

    def project(values):
        return jnp.einsum("rd,fd->rf", values, piece, preferred_element_type=jnp.float32).astype(
            jnp.bfloat16
        )

    arrived = lax.ppermute(project(rows_there), "core", twin)
    partial = project(rows_here).astype(jnp.float32) + arrived.astype(jnp.float32)
    partial = partial.astype(jnp.bfloat16).reshape(owners, half_rows // owners, hidden_units)
    gathered = lax.all_to_all(partial, OWNERS, 0, 0)
    gathered = gathered.reshape((2, owners // 2) + gathered.shape[1:])
    near = jnp.sum(gathered.astype(jnp.float32), axis=1).astype(jnp.bfloat16)
    far = lax.ppermute(near, "zh", twin)
    total = near.astype(jnp.float32) + far.astype(jnp.float32)
    pre_sum = total[0]
    grad_hidden = total[1].astype(jnp.bfloat16).astype(jnp.float32)
    logistic = jax.nn.sigmoid(pre_sum)
    hidden = (pre_sum * logistic).astype(jnp.bfloat16)
    grad_pre = (grad_hidden * logistic * (1.0 + pre_sum * (1.0 - logistic))).astype(jnp.bfloat16)

    answer = jnp.concatenate(
        [
            jnp.broadcast_to(grad_pre[None], (owners // 2,) + grad_pre.shape),
            jnp.broadcast_to(hidden[None], (owners // 2,) + hidden.shape),
        ]
    )
    left_here = lax.all_to_all(answer, OWNERS, 0, 0).reshape(half_rows, hidden_units)
    left_there = lax.ppermute(left_here, "core", twin)
    grads = jnp.einsum(
        "rf,rd->fd",
        jnp.concatenate([left_here, left_there]),
        jnp.concatenate([rows_here, rows_there]),
        preferred_element_type=jnp.float32,
    )
    return grads.astype(jnp.bfloat16)[None]


def solution(mesh):
    fine = Mesh(
        np.asarray(mesh.devices).reshape(2, 2, 8, 2, 4, 2),
        ("half", "yl", "zl", "zh", "x", "core"),
    )
    placed = (
        P(None, SECTION, TENSOR),
        P(None, SECTION, TENSOR),
        P(),
        P(SECTION, None, TENSOR),
    )
    return jax.shard_map(
        local, mesh=fine, in_specs=placed, out_specs=P(SECTION, None, TENSOR), check_vma=False
    )
```

```python
import jax
import jax.numpy as jnp
import numpy as np
from jax import lax
from jax.experimental import pallas as pl
from jax.experimental.pallas import tpu as pltpu
from jax.sharding import Mesh, PartitionSpec as P

SECTION = ("half", "yl", "zl")
TENSOR = ("zh", "x", "core")
ROOT = 4
OWNERS = ("half", "x")


def pack_kernel(plan_ref, inputs_ref, cotangent_ref, out_ref):
    batches = inputs_ref.shape[0]
    half = out_ref.shape[0] // 2
    entering = jnp.concatenate(
        [inputs_ref[plan_ref[k]].astype(jnp.float32) for k in range(batches)], axis=0
    )
    returning = jnp.concatenate(
        [cotangent_ref[k].astype(jnp.float32) for k in range(batches)], axis=0
    )
    for first, rows in ((0, entering), (half, returning)):
        rows = rows.astype(out_ref.dtype)
        out_ref[pl.ds(first, half)] = jnp.broadcast_to(rows[None], (half,) + rows.shape)


def pack(plan, inputs, cotangent, sections):
    batches, tokens, width = inputs.shape
    return pl.pallas_call(
        pack_kernel,
        out_shape=jax.ShapeDtypeStruct((sections, batches * tokens, width), inputs.dtype),
        in_specs=[
            pl.BlockSpec(memory_space=pltpu.SMEM),
            pl.BlockSpec(memory_space=pltpu.VMEM),
            pl.BlockSpec(memory_space=pltpu.VMEM),
        ],
        out_specs=pl.BlockSpec(memory_space=pltpu.VMEM),
    )(plan, inputs, cotangent)


def local(inputs, cotangent, plan, weights):
    piece = weights[0]
    hidden_units, width = piece.shape
    sections = lax.axis_size(SECTION)
    owners = lax.axis_size(OWNERS)
    core = lax.axis_index("core")
    twin = [(0, 1), (1, 0)]

    order = [h * 16 + y * 8 + (z + ROOT) % 8 for h in range(2) for y in range(2) for z in range(8)]
    rows = lax.all_to_all(pack(plan, inputs, cotangent, sections), SECTION, 0, 0, axis_index_groups=[order])
    rows = rows.reshape(2, -1, width)
    half_rows = rows.shape[1]
    rows_here = lax.dynamic_index_in_dim(rows, core, 0, keepdims=False)
    rows_there = lax.dynamic_index_in_dim(rows, 1 - core, 0, keepdims=False)

    def project(values):
        return jnp.einsum("rd,fd->rf", values, piece, preferred_element_type=jnp.float32).astype(
            jnp.bfloat16
        )

    arrived = lax.ppermute(project(rows_there), "core", twin)
    partial = project(rows_here).astype(jnp.float32) + arrived.astype(jnp.float32)
    partial = partial.astype(jnp.bfloat16).reshape(owners, half_rows // owners, hidden_units)
    gathered = lax.all_to_all(partial, OWNERS, 0, 0)
    gathered = gathered.reshape((2, owners // 2) + gathered.shape[1:])
    near = jnp.sum(gathered.astype(jnp.float32), axis=1).astype(jnp.bfloat16)
    far = lax.ppermute(near, "zh", twin)
    total = near.astype(jnp.float32) + far.astype(jnp.float32)
    pre_sum = total[0]
    grad_hidden = total[1].astype(jnp.bfloat16).astype(jnp.float32)
    logistic = jax.nn.sigmoid(pre_sum)
    hidden = (pre_sum * logistic).astype(jnp.bfloat16)
    grad_pre = (grad_hidden * logistic * (1.0 + pre_sum * (1.0 - logistic))).astype(jnp.bfloat16)

    answer = jnp.concatenate(
        [
            jnp.broadcast_to(grad_pre[None], (owners // 2,) + grad_pre.shape),
            jnp.broadcast_to(hidden[None], (owners // 2,) + hidden.shape),
        ]
    )
    left_here = lax.all_to_all(answer, OWNERS, 0, 0).reshape(half_rows, hidden_units)
    left_there = lax.ppermute(left_here, "core", twin)
    grads = jnp.einsum(
        "rf,rd->fd",
        jnp.concatenate([left_here, left_there]),
        jnp.concatenate([rows_here, rows_there]),
        preferred_element_type=jnp.float32,
    )
    return grads.astype(jnp.bfloat16)[None]


def solution(mesh):
    fine = Mesh(
        np.asarray(mesh.devices).reshape(2, 2, 8, 2, 4, 2),
        ("half", "yl", "zl", "zh", "x", "core"),
    )
    placed = (
        P(None, SECTION, TENSOR),
        P(None, SECTION, TENSOR),
        P(),
        P(SECTION, None, TENSOR),
    )
    return jax.shard_map(
        local, mesh=fine, in_specs=placed, out_specs=P(SECTION, None, TENSOR), check_vma=False
    )
```

```python
import jax
import jax.numpy as jnp
import numpy as np
from jax import lax
from jax.experimental import pallas as pl
from jax.experimental.pallas import tpu as pltpu
from jax.sharding import Mesh, PartitionSpec as P

SECTION = ("half", "yl", "zl")
TENSOR = ("zh", "x", "core")
OWNERS = ("half", "x")
TILES = 4


def pack_kernel(plan_ref, inputs_ref, cotangent_ref, out_ref):
    batches = inputs_ref.shape[0]
    half = out_ref.shape[0] // 2
    entering = jnp.concatenate(
        [inputs_ref[plan_ref[k]].astype(jnp.float32) for k in range(batches)], axis=0
    )
    returning = jnp.concatenate(
        [cotangent_ref[k].astype(jnp.float32) for k in range(batches)], axis=0
    )
    for first, rows in ((0, entering), (half, returning)):
        rows = rows.astype(out_ref.dtype)
        out_ref[pl.ds(first, half)] = jnp.broadcast_to(rows[None], (half,) + rows.shape)


def pack(plan, inputs, cotangent, sections):
    batches, tokens, width = inputs.shape
    return pl.pallas_call(
        pack_kernel,
        out_shape=jax.ShapeDtypeStruct((sections, batches * tokens, width), inputs.dtype),
        in_specs=[
            pl.BlockSpec(memory_space=pltpu.SMEM),
            pl.BlockSpec(memory_space=pltpu.VMEM),
            pl.BlockSpec(memory_space=pltpu.VMEM),
        ],
        out_specs=pl.BlockSpec(memory_space=pltpu.VMEM),
    )(plan, inputs, cotangent)


def gradient_kernel(side_ref, left_ref, rows_ref, *refs):
    out_ref = refs[-1]
    tile = out_ref.shape[1]
    first = pl.multiple_of(pl.program_id(0) * tile, tile)
    out_ref[0] = jnp.dot(
        left_ref[pl.ds(first, tile), :], rows_ref[...], preferred_element_type=jnp.float32
    ).astype(out_ref.dtype)


def gradient(side, left, rows, done=None):
    units, row_count = left.shape
    width = rows.shape[1]
    tile = units // TILES
    operands = (side, left, rows) + (() if done is None else (done,))
    return pl.pallas_call(
        gradient_kernel,
        out_shape=jax.ShapeDtypeStruct((2, units, width), left.dtype),
        grid_spec=pltpu.PrefetchScalarGridSpec(
            num_scalar_prefetch=1,
            grid=(TILES,),
            in_specs=[
                pl.BlockSpec(memory_space=pltpu.VMEM),
                pl.BlockSpec(memory_space=pltpu.VMEM),
            ]
            + ([] if done is None else [pl.BlockSpec(memory_space=pl.ANY)]),
            out_specs=pl.BlockSpec((1, tile, width), lambda i, side_ref: (side_ref[0], i, 0)),
        ),
        input_output_aliases={} if done is None else {3: 0},
        cost_estimate=pl.CostEstimate(
            flops=2 * units * row_count * width,
            bytes_accessed=2 * units * (row_count + width),
            transcendentals=0,
        ),
    )(*operands)


def local(inputs, cotangent, plan, weights):
    hidden_units, width = weights.shape[1:]
    sections = lax.axis_size(SECTION)
    depth = lax.axis_size("zl")
    owners = lax.axis_size(OWNERS)
    core = lax.axis_index("core")
    twin = [(0, 1), (1, 0)]

    order = [
        first + (z + depth // 2) % depth for first in range(0, sections, depth) for z in range(depth)
    ]
    rows = lax.all_to_all(
        pack(plan, inputs, cotangent, sections), SECTION, 0, 0, axis_index_groups=[order]
    ).reshape(-1, width)
    row_count = rows.shape[0]

    piece = weights.reshape(2, hidden_units // 2, width)
    piece_own = lax.dynamic_index_in_dim(piece, core, 0, keepdims=False)
    piece_twin = lax.ppermute(
        lax.dynamic_index_in_dim(piece, 1 - core, 0, keepdims=False), "core", twin
    )
    rows_twin = lax.ppermute(rows, "core", twin)

    def project(values, matrix):
        return jnp.einsum("fd,rd->fr", matrix, values, preferred_element_type=jnp.float32)

    near_part = lax.optimization_barrier(project(rows, piece_own).astype(jnp.bfloat16))
    far_part = lax.optimization_barrier(project(rows_twin, piece_twin).astype(jnp.bfloat16))
    partial = near_part.astype(jnp.float32) + far_part.astype(jnp.float32)
    partial = partial.astype(jnp.bfloat16).reshape(owners, -1, row_count)
    gathered = lax.all_to_all(partial, OWNERS, 0, 0)
    gathered = gathered.reshape((2, owners // 2) + gathered.shape[1:])
    near = jnp.sum(gathered.astype(jnp.float32), axis=1).astype(jnp.bfloat16)
    both = lax.all_gather(near, "zh")
    total = both[0].astype(jnp.float32) + both[1].astype(jnp.float32)
    pre_sum = total[0]
    grad_hidden = total[1].astype(jnp.bfloat16).astype(jnp.float32)
    logistic = jax.nn.sigmoid(pre_sum)
    hidden = (pre_sum * logistic).astype(jnp.bfloat16)
    grad_pre = (grad_hidden * logistic * (1.0 + pre_sum * (1.0 - logistic))).astype(jnp.bfloat16)

    answer = jnp.concatenate(
        [
            jnp.broadcast_to(grad_pre[None], (owners // 2,) + grad_pre.shape),
            jnp.broadcast_to(hidden[None], (owners // 2,) + hidden.shape),
        ]
    )
    left = lax.all_to_all(answer, OWNERS, 0, 0).reshape(-1, row_count)
    whole = lax.all_gather(left, "core", axis=0, tiled=True)
    grads = jnp.einsum("fr,rd->fd", whole, rows, preferred_element_type=jnp.float32)
    grads = grads.astype(jnp.bfloat16)
    return grads.reshape(1, hidden_units, width)


def solution(mesh):
    fine = Mesh(
        np.asarray(mesh.devices).reshape(2, 2, 8, 2, 4, 2),
        ("half", "yl", "zl", "zh", "x", "core"),
    )
    placed = (
        P(None, SECTION, TENSOR),
        P(None, SECTION, TENSOR),
        P(),
        P(SECTION, None, TENSOR),
    )
    return jax.shard_map(
        local, mesh=fine, in_specs=placed, out_specs=P(SECTION, None, TENSOR), check_vma=False
    )
```

```python
import jax
import jax.numpy as jnp
import numpy as np
from jax import lax
from jax.experimental import pallas as pl
from jax.experimental.pallas import tpu as pltpu
from jax.sharding import Mesh, PartitionSpec as P

SECTION = ("half", "yl", "zl")
TENSOR = ("zh", "x", "core")
OWNERS = ("half", "x")
TILES = 4


def pack_kernel(plan_ref, inputs_ref, cotangent_ref, out_ref):
    batches = inputs_ref.shape[0]
    half = out_ref.shape[0] // 2
    returning = jnp.concatenate(
        [cotangent_ref[k].astype(jnp.float32) for k in range(batches)], axis=0
    ).astype(out_ref.dtype)
    entering = jnp.concatenate(
        [inputs_ref[plan_ref[k]].astype(jnp.float32) for k in range(batches)], axis=0
    ).astype(out_ref.dtype)
    for i in range(half):
        out_ref[i] = returning
        out_ref[half + i] = entering


def pack(plan, inputs, cotangent, sections):
    batches, tokens, width = inputs.shape
    return pl.pallas_call(
        pack_kernel,
        out_shape=jax.ShapeDtypeStruct((sections, batches * tokens, width), inputs.dtype),
        in_specs=[
            pl.BlockSpec(memory_space=pltpu.SMEM),
            pl.BlockSpec(memory_space=pltpu.VMEM),
            pl.BlockSpec(memory_space=pltpu.VMEM),
        ],
        out_specs=pl.BlockSpec(memory_space=pltpu.VMEM),
    )(plan, inputs, cotangent)


def gradient_kernel(left_ref, rows_ref, out_ref, held_ref, sems):
    tile = left_ref.shape[0] // 4
    copies = []
    for i in range(4):
        block = pl.ds(i * tile, tile)
        held_ref[block, :] = jnp.dot(
            left_ref[block, :], rows_ref[...], preferred_element_type=jnp.float32
        ).astype(held_ref.dtype)
        copies.append(pltpu.make_async_copy(held_ref.at[block], out_ref.at[block], sems.at[i]))
        copies[-1].start()
    for copy in copies:
        copy.wait()


def gradient(left, rows):
    units = left.shape[0]
    width = rows.shape[1]
    return pl.pallas_call(
        gradient_kernel,
        out_shape=jax.ShapeDtypeStruct((units, width), left.dtype),
        in_specs=[pl.BlockSpec(memory_space=pltpu.VMEM), pl.BlockSpec(memory_space=pltpu.VMEM)],
        out_specs=pl.BlockSpec(memory_space=pl.ANY),
        scratch_shapes=[pltpu.VMEM((units, width), left.dtype), pltpu.SemaphoreType.DMA((4,))],
        compiler_params=pltpu.CompilerParams(vmem_limit_bytes=8 << 20),
    )(left, rows)


def local(inputs, cotangent, plan, weights):
    hidden_units, width = weights.shape[1:]
    sections = lax.axis_size(SECTION)
    depth = lax.axis_size("zl")
    owners = lax.axis_size(OWNERS)
    core = lax.axis_index("core")
    twin = [(0, 1), (1, 0)]

    order = [
        first + (z + depth // 2) % depth
        for first in (*range(sections // 2, sections, depth), *range(0, sections // 2, depth))
        for z in range(depth)
    ]
    owner_order = list(range(owners))[::-1]
    rows = lax.all_to_all(
        pack(plan, inputs, cotangent, sections), SECTION, 0, 0, axis_index_groups=[order]
    ).reshape(-1, width)
    row_count = rows.shape[0]

    piece = weights.reshape(2, hidden_units // 2, width)
    piece_own = lax.dynamic_index_in_dim(piece, core, 0, keepdims=False)
    piece_twin = lax.ppermute(
        lax.dynamic_index_in_dim(piece, 1 - core, 0, keepdims=False), "core", twin
    )
    rows_twin = lax.ppermute(rows, "core", twin)

    def project(values, matrix):
        return jnp.einsum("fd,rd->fr", matrix, values, preferred_element_type=jnp.float32)

    near_part = lax.optimization_barrier(project(rows, piece_own).astype(jnp.bfloat16))
    far_part = lax.optimization_barrier(project(rows_twin, piece_twin).astype(jnp.bfloat16))
    partial = near_part.astype(jnp.float32) + far_part.astype(jnp.float32)
    partial = partial.astype(jnp.bfloat16).reshape(owners, -1, row_count)
    gathered = lax.all_to_all(partial, OWNERS, 0, 0, axis_index_groups=[owner_order])
    gathered = gathered.reshape((2, owners // 2) + gathered.shape[1:])
    near = jnp.sum(gathered.astype(jnp.float32), axis=1).astype(jnp.bfloat16)
    both = lax.all_gather(near, "zh")
    total = both[0].astype(jnp.float32) + both[1].astype(jnp.float32)
    pre_sum = total[1]
    grad_hidden = total[0].astype(jnp.bfloat16).astype(jnp.float32)
    logistic = jax.nn.sigmoid(pre_sum)
    hidden = (pre_sum * logistic).astype(jnp.bfloat16)
    grad_pre = (grad_hidden * logistic * (1.0 + pre_sum * (1.0 - logistic))).astype(jnp.bfloat16)

    answer = jnp.concatenate(
        [
            jnp.broadcast_to(hidden[None], (owners // 2,) + hidden.shape),
            jnp.broadcast_to(grad_pre[None], (owners // 2,) + grad_pre.shape),
        ]
    )
    left = lax.all_to_all(answer, OWNERS, 0, 0, axis_index_groups=[owner_order]).reshape(-1, row_count)
    whole = lax.all_gather(left, "core", axis=0, tiled=True)
    grads = gradient(whole, rows)
    return grads.reshape(1, hidden_units, width)


def solution(mesh):
    fine = Mesh(
        np.asarray(mesh.devices).reshape(2, 2, 8, 2, 4, 2),
        ("half", "yl", "zl", "zh", "x", "core"),
    )
    placed = (
        P(None, SECTION, TENSOR),
        P(None, SECTION, TENSOR),
        P(),
        P(SECTION, None, TENSOR),
    )
    return jax.shard_map(
        local, mesh=fine, in_specs=placed, out_specs=P(SECTION, None, TENSOR), check_vma=False
    )
```

```python
import jax
import jax.numpy as jnp
import numpy as np
from jax import lax
from jax.experimental import pallas as pl
from jax.experimental.pallas import tpu as pltpu
from jax.sharding import Mesh, PartitionSpec as P

SECTION = ("half", "yl", "zl")
TENSOR = ("zh", "x", "core")
OWNERS = ("half", "x")
TILES = 4


def pack_kernel(plan_ref, inputs_ref, cotangent_ref, out_ref):
    batches = inputs_ref.shape[0]
    half = out_ref.shape[0] // 2
    returning = jnp.concatenate(
        [cotangent_ref[k].astype(jnp.float32) for k in range(batches)], axis=0
    ).astype(out_ref.dtype)
    entering = jnp.concatenate(
        [inputs_ref[plan_ref[k]].astype(jnp.float32) for k in range(batches)], axis=0
    ).astype(out_ref.dtype)
    for i in range(half):
        out_ref[i] = returning
        out_ref[half + i] = entering


def pack(plan, inputs, cotangent, sections):
    batches, tokens, width = inputs.shape
    return pl.pallas_call(
        pack_kernel,
        out_shape=jax.ShapeDtypeStruct((sections, batches * tokens, width), inputs.dtype),
        in_specs=[
            pl.BlockSpec(memory_space=pltpu.SMEM),
            pl.BlockSpec(memory_space=pltpu.VMEM),
            pl.BlockSpec(memory_space=pltpu.VMEM),
        ],
        out_specs=pl.BlockSpec(memory_space=pltpu.VMEM),
    )(plan, inputs, cotangent)


def gradient_kernel(left_ref, rows_ref, out_ref, held_ref, sems):
    tile = left_ref.shape[0] // 4
    copies = []
    for i in range(4):
        block = pl.ds(i * tile, tile)
        held_ref[block, :] = jnp.dot(
            left_ref[block, :], rows_ref[...], preferred_element_type=jnp.float32
        ).astype(held_ref.dtype)
        copies.append(pltpu.make_async_copy(held_ref.at[block], out_ref.at[block], sems.at[i]))
        copies[-1].start()
    for copy in copies:
        copy.wait()


def gradient(left, rows):
    units = left.shape[0]
    width = rows.shape[1]
    return pl.pallas_call(
        gradient_kernel,
        out_shape=jax.ShapeDtypeStruct((units, width), left.dtype),
        in_specs=[pl.BlockSpec(memory_space=pltpu.VMEM), pl.BlockSpec(memory_space=pltpu.VMEM)],
        out_specs=pl.BlockSpec(memory_space=pl.ANY),
        scratch_shapes=[pltpu.VMEM((units, width), left.dtype), pltpu.SemaphoreType.DMA((4,))],
        compiler_params=pltpu.CompilerParams(vmem_limit_bytes=8 << 20),
    )(left, rows)


def local(inputs, cotangent, plan, weights):
    hidden_units, width = weights.shape[1:]
    sections = lax.axis_size(SECTION)
    depth = lax.axis_size("zl")
    owners = lax.axis_size(OWNERS)
    core = lax.axis_index("core")
    twin = [(0, 1), (1, 0)]

    order = [
        first + (z + depth // 2) % depth
        for first in (*range(sections // 2, sections, depth), *range(0, sections // 2, depth))
        for z in range(depth)
    ]
    owner_order = [half * (owners // 2) + x for x in reversed(range(owners // 2)) for half in (1, 0)]
    rows = lax.all_to_all(
        pack(plan, inputs, cotangent, sections), SECTION, 0, 0, axis_index_groups=[order]
    ).reshape(-1, width)
    row_count = rows.shape[0]

    piece = weights.reshape(2, hidden_units // 2, width)
    piece_own = lax.dynamic_index_in_dim(piece, core, 0, keepdims=False)
    piece_twin = lax.ppermute(
        lax.dynamic_index_in_dim(piece, 1 - core, 0, keepdims=False), "core", twin
    )
    rows_twin = lax.ppermute(rows, "core", twin)

    def project(values, matrix):
        return jnp.einsum("fd,rd->fr", matrix, values, preferred_element_type=jnp.float32)

    near_part = lax.optimization_barrier(project(rows, piece_own).astype(jnp.bfloat16))
    far_part = lax.optimization_barrier(project(rows_twin, piece_twin).astype(jnp.bfloat16))
    partial = near_part.astype(jnp.float32) + far_part.astype(jnp.float32)
    partial = partial.astype(jnp.bfloat16).reshape(owners, -1, row_count)
    gathered = lax.all_to_all(partial, OWNERS, 0, 0, axis_index_groups=[owner_order])
    gathered = gathered.reshape((owners // 2, 2) + gathered.shape[1:])
    near = jnp.sum(gathered.astype(jnp.float32), axis=0).astype(jnp.bfloat16)
    both = lax.all_gather(near, "zh")
    total = both[0].astype(jnp.float32) + both[1].astype(jnp.float32)
    pre_sum = total[1]
    grad_hidden = total[0].astype(jnp.bfloat16).astype(jnp.float32)
    logistic = jax.nn.sigmoid(pre_sum)
    hidden = (pre_sum * logistic).astype(jnp.bfloat16)
    grad_pre = (grad_hidden * logistic * (1.0 + pre_sum * (1.0 - logistic))).astype(jnp.bfloat16)

    answer = jnp.stack([hidden, grad_pre])
    answer = jnp.broadcast_to(answer[None], (owners // 2,) + answer.shape)
    answer = answer.reshape((owners,) + hidden.shape)
    left = lax.all_to_all(answer, OWNERS, 0, 0, axis_index_groups=[owner_order]).reshape(-1, row_count)
    whole = lax.all_gather(left, "core", axis=0, tiled=True)
    grads = gradient(whole, rows)
    return grads.reshape(1, hidden_units, width)


def solution(mesh):
    fine = Mesh(
        np.asarray(mesh.devices).reshape(2, 2, 8, 2, 4, 2),
        ("half", "yl", "zl", "zh", "x", "core"),
    )
    placed = (
        P(None, SECTION, TENSOR),
        P(None, SECTION, TENSOR),
        P(),
        P(SECTION, None, TENSOR),
    )
    return jax.shard_map(
        local, mesh=fine, in_specs=placed, out_specs=P(SECTION, None, TENSOR), check_vma=False
    )
```

```python
import jax
import jax.numpy as jnp
import numpy as np
from jax import lax
from jax.experimental import pallas as pl
from jax.experimental.pallas import tpu as pltpu
from jax.sharding import Mesh, PartitionSpec as P

SECTION = ("half", "yl", "zl")
TENSOR = ("zh", "x", "core")
OWNERS = ("half", "x")
TILES = 4


def pack_kernel(plan_ref, inputs_ref, cotangent_ref, out_ref):
    batches = inputs_ref.shape[0]
    half = out_ref.shape[0] // 2
    returning = jnp.concatenate(
        [cotangent_ref[k].astype(jnp.float32) for k in range(batches)], axis=0
    ).astype(out_ref.dtype)
    entering = jnp.concatenate(
        [inputs_ref[plan_ref[k]].astype(jnp.float32) for k in range(batches)], axis=0
    ).astype(out_ref.dtype)
    for i in range(half):
        out_ref[i] = returning
        out_ref[half + i] = entering


def pack(plan, inputs, cotangent, sections):
    batches, tokens, width = inputs.shape
    return pl.pallas_call(
        pack_kernel,
        out_shape=jax.ShapeDtypeStruct((sections, batches * tokens, width), inputs.dtype),
        in_specs=[
            pl.BlockSpec(memory_space=pltpu.SMEM),
            pl.BlockSpec(memory_space=pltpu.VMEM),
            pl.BlockSpec(memory_space=pltpu.VMEM),
        ],
        out_specs=pl.BlockSpec(memory_space=pltpu.VMEM),
    )(plan, inputs, cotangent)


def gradient_kernel(left_ref, rows_ref, out_ref, held_ref, sems):
    tile = left_ref.shape[0] // 4
    copies = []
    for i in range(4):
        block = pl.ds(i * tile, tile)
        held_ref[block, :] = jnp.dot(
            left_ref[block, :], rows_ref[...], preferred_element_type=jnp.float32
        ).astype(held_ref.dtype)
        copies.append(pltpu.make_async_copy(held_ref.at[block], out_ref.at[block], sems.at[i]))
        copies[-1].start()
    for copy in copies:
        copy.wait()


def gradient(left, rows):
    units = left.shape[0]
    width = rows.shape[1]
    return pl.pallas_call(
        gradient_kernel,
        out_shape=jax.ShapeDtypeStruct((units, width), left.dtype),
        in_specs=[pl.BlockSpec(memory_space=pltpu.VMEM), pl.BlockSpec(memory_space=pltpu.VMEM)],
        out_specs=pl.BlockSpec(memory_space=pl.ANY),
        scratch_shapes=[pltpu.VMEM((units, width), left.dtype), pltpu.SemaphoreType.DMA((4,))],
        compiler_params=pltpu.CompilerParams(vmem_limit_bytes=8 << 20),
    )(left, rows)


def local(inputs, cotangent, plan, weights):
    hidden_units, width = weights.shape[1:]
    sections = lax.axis_size(SECTION)
    depth = lax.axis_size("zl")
    owners = lax.axis_size(OWNERS)
    core = lax.axis_index("core")
    twin = [(0, 1), (1, 0)]

    order = [
        first + (z + depth // 2) % depth
        for first in (*range(sections // 2, sections, depth), *range(0, sections // 2, depth))
        for z in range(depth)
    ]
    owner_order = [half * (owners // 2) + x for x in reversed(range(owners // 2)) for half in (1, 0)]
    rows = lax.all_to_all(
        pack(plan, inputs, cotangent, sections), SECTION, 0, 0, axis_index_groups=[order]
    ).reshape(-1, width)
    row_count = rows.shape[0]

    piece = weights.reshape(2, hidden_units // 2, width)
    piece_own, piece_sent = lax.optimization_barrier(
        (
            lax.dynamic_index_in_dim(piece, core, 0, keepdims=False),
            lax.dynamic_index_in_dim(piece, 1 - core, 0, keepdims=False),
        )
    )
    piece_twin = lax.ppermute(piece_sent, "core", twin)
    both_rows = lax.all_gather(rows, "core")
    rows_twin = lax.optimization_barrier(jnp.where(core == 0, both_rows[1], both_rows[0]))

    def project(values, matrix):
        return jnp.einsum("fd,rd->fr", matrix, values, preferred_element_type=jnp.float32)

    pieces = lax.optimization_barrier(jnp.concatenate([piece_own, piece_twin], axis=1))
    partial = project(jnp.concatenate([rows, rows_twin], axis=1), pieces)
    partial = partial.astype(jnp.bfloat16).reshape(owners, -1, row_count)
    gathered = lax.all_to_all(partial, OWNERS, 0, 0, axis_index_groups=[owner_order])
    gathered = gathered.reshape((owners // 2, 2) + gathered.shape[1:])
    near = jnp.sum(gathered.astype(jnp.float32), axis=0).astype(jnp.bfloat16)
    both = lax.all_gather(near, "zh")
    total = both[0].astype(jnp.float32) + both[1].astype(jnp.float32)
    pre_sum = total[1]
    grad_hidden = total[0].astype(jnp.bfloat16).astype(jnp.float32)
    logistic = jax.nn.sigmoid(pre_sum)
    hidden = (pre_sum * logistic).astype(jnp.bfloat16)
    grad_pre = (grad_hidden * logistic * (1.0 + pre_sum * (1.0 - logistic))).astype(jnp.bfloat16)

    answer = jnp.stack([hidden, grad_pre])
    answer = jnp.broadcast_to(answer[None], (owners // 2,) + answer.shape)
    answer = answer.reshape((owners,) + hidden.shape)
    left = lax.all_to_all(answer, OWNERS, 0, 0, axis_index_groups=[owner_order]).reshape(-1, row_count)
    whole = lax.all_gather(left, "core", axis=0, tiled=True)
    grads = gradient(whole, rows)
    return grads.reshape(1, hidden_units, width)


def solution(mesh):
    fine = Mesh(
        np.asarray(mesh.devices).reshape(2, 2, 8, 2, 4, 2),
        ("half", "yl", "zl", "zh", "x", "core"),
    )
    placed = (
        P(None, SECTION, TENSOR),
        P(None, SECTION, TENSOR),
        P(),
        P(SECTION, None, TENSOR),
    )
    return jax.shard_map(
        local, mesh=fine, in_specs=placed, out_specs=P(SECTION, None, TENSOR), check_vma=False
    )
```

```python
import jax
import jax.numpy as jnp
import numpy as np
from jax import lax
from jax.experimental import pallas as pl
from jax.experimental.pallas import tpu as pltpu
from jax.sharding import Mesh, PartitionSpec as P

SECTION = ("half", "yl", "zl")
TENSOR = ("zh", "x", "core")
OWNERS = ("half", "x")
TILES = 4


def pack_kernel(plan_ref, inputs_ref, cotangent_ref, out_ref):
    batches = inputs_ref.shape[0]
    half = out_ref.shape[0] // 2
    returning = jnp.concatenate(
        [cotangent_ref[k].astype(jnp.float32) for k in range(batches)], axis=0
    ).astype(out_ref.dtype)
    entering = jnp.concatenate(
        [inputs_ref[plan_ref[k]].astype(jnp.float32) for k in range(batches)], axis=0
    ).astype(out_ref.dtype)
    for i in range(half):
        out_ref[i] = returning
        out_ref[half + i] = entering


def pack(plan, inputs, cotangent, sections):
    batches, tokens, width = inputs.shape
    return pl.pallas_call(
        pack_kernel,
        out_shape=jax.ShapeDtypeStruct((sections, batches * tokens, width), inputs.dtype),
        in_specs=[
            pl.BlockSpec(memory_space=pltpu.SMEM),
            pl.BlockSpec(memory_space=pltpu.VMEM),
            pl.BlockSpec(memory_space=pltpu.VMEM),
        ],
        out_specs=pl.BlockSpec(memory_space=pltpu.VMEM),
    )(plan, inputs, cotangent)


def gradient_kernel(left_ref, rows_ref, out_ref, held_ref, sems):
    tile = left_ref.shape[0] // 4
    copies = []
    for i in range(4):
        block = pl.ds(i * tile, tile)
        held_ref[block, :] = jnp.dot(
            left_ref[block, :], rows_ref[...], preferred_element_type=jnp.float32
        ).astype(held_ref.dtype)
        copies.append(pltpu.make_async_copy(held_ref.at[block], out_ref.at[block], sems.at[i]))
        copies[-1].start()
    for copy in copies:
        copy.wait()


def gradient(left, rows):
    units = left.shape[0]
    width = rows.shape[1]
    return pl.pallas_call(
        gradient_kernel,
        out_shape=jax.ShapeDtypeStruct((units, width), left.dtype),
        in_specs=[pl.BlockSpec(memory_space=pltpu.VMEM), pl.BlockSpec(memory_space=pltpu.VMEM)],
        out_specs=pl.BlockSpec(memory_space=pl.ANY),
        scratch_shapes=[pltpu.VMEM((units, width), left.dtype), pltpu.SemaphoreType.DMA((4,))],
        compiler_params=pltpu.CompilerParams(vmem_limit_bytes=8 << 20),
    )(left, rows)


def local(inputs, cotangent, plan, weights):
    hidden_units, width = weights.shape[1:]
    sections = lax.axis_size(SECTION)
    depth = lax.axis_size("zl")
    owners = lax.axis_size(OWNERS)
    core = lax.axis_index("core")
    twin = [(0, 1), (1, 0)]

    order = [
        first + (z + depth // 2) % depth
        for first in (*range(sections // 2, sections, depth), *range(0, sections // 2, depth))
        for z in range(depth)
    ]
    owner_order = [half * (owners // 2) + x for x in (3, 1, 2, 0) for half in (1, 0)]
    rows = lax.all_to_all(
        pack(plan, inputs, cotangent, sections), SECTION, 0, 0, axis_index_groups=[order]
    ).reshape(-1, width)
    row_count = rows.shape[0]

    piece = weights.reshape(2, hidden_units // 2, width)
    piece_own, piece_sent = lax.optimization_barrier(
        (
            lax.dynamic_index_in_dim(piece, core, 0, keepdims=False),
            lax.dynamic_index_in_dim(piece, 1 - core, 0, keepdims=False),
        )
    )
    piece_twin = lax.ppermute(piece_sent, "core", twin)
    both_rows = lax.all_gather(rows, "core")
    rows_twin = lax.optimization_barrier(jnp.where(core == 0, both_rows[1], both_rows[0]))

    def project(values, matrix):
        return jnp.einsum("fd,rd->fr", matrix, values, preferred_element_type=jnp.float32)

    pieces = lax.optimization_barrier(jnp.concatenate([piece_own, piece_twin], axis=1))
    partial = project(jnp.concatenate([rows, rows_twin], axis=1), pieces)
    partial = partial.astype(jnp.bfloat16).reshape(owners, -1, row_count)
    gathered = lax.all_to_all(partial, OWNERS, 0, 0, axis_index_groups=[owner_order])
    gathered = gathered.reshape((owners // 2, 2) + gathered.shape[1:])
    near = jnp.sum(gathered.astype(jnp.float32), axis=0).astype(jnp.bfloat16)
    both = lax.all_gather(near, "zh")
    total = both[0].astype(jnp.float32) + both[1].astype(jnp.float32)
    pre_sum = total[1]
    grad_hidden = total[0].astype(jnp.bfloat16).astype(jnp.float32)
    logistic = jax.nn.sigmoid(pre_sum)
    hidden = (pre_sum * logistic).astype(jnp.bfloat16)
    grad_pre = (grad_hidden * logistic * (1.0 + pre_sum * (1.0 - logistic))).astype(jnp.bfloat16)

    answer = jnp.stack([hidden, grad_pre])
    answer = jnp.broadcast_to(answer[None], (owners // 2,) + answer.shape)
    answer = answer.reshape((owners,) + hidden.shape)
    left = lax.all_to_all(answer, OWNERS, 0, 0, axis_index_groups=[owner_order]).reshape(-1, row_count)
    whole = lax.all_gather(left, "core", axis=0, tiled=True)
    grads = gradient(whole, rows)
    return grads.reshape(1, hidden_units, width)


def solution(mesh):
    fine = Mesh(
        np.asarray(mesh.devices).reshape(2, 2, 8, 2, 4, 2),
        ("half", "yl", "zl", "zh", "x", "core"),
    )
    placed = (
        P(None, SECTION, TENSOR),
        P(None, SECTION, TENSOR),
        P(),
        P(SECTION, None, TENSOR),
    )
    return jax.shard_map(
        local, mesh=fine, in_specs=placed, out_specs=P(SECTION, None, TENSOR), check_vma=False
    )
```

```python
import jax
import jax.numpy as jnp
import numpy as np
from jax import lax
from jax.experimental import pallas as pl
from jax.experimental.pallas import tpu as pltpu
from jax.sharding import Mesh, PartitionSpec as P

SECTION = ("half", "yl", "zl")
TENSOR = ("zh", "x", "core")
OWNERS = ("half", "x")
TILES = 8


def pack_kernel(plan_ref, inputs_ref, cotangent_ref, out_ref):
    batches = inputs_ref.shape[0]
    half = out_ref.shape[0] // 2
    returning = jnp.concatenate(
        [cotangent_ref[k].astype(jnp.float32) for k in range(batches)], axis=0
    ).astype(out_ref.dtype)
    entering = jnp.concatenate(
        [inputs_ref[plan_ref[k]].astype(jnp.float32) for k in range(batches)], axis=0
    ).astype(out_ref.dtype)
    for i in range(half):
        out_ref[i] = returning
        out_ref[half + i] = entering


def pack(plan, inputs, cotangent, sections):
    batches, tokens, width = inputs.shape
    return pl.pallas_call(
        pack_kernel,
        out_shape=jax.ShapeDtypeStruct((sections, batches * tokens, width), inputs.dtype),
        in_specs=[
            pl.BlockSpec(memory_space=pltpu.SMEM),
            pl.BlockSpec(memory_space=pltpu.VMEM),
            pl.BlockSpec(memory_space=pltpu.VMEM),
        ],
        out_specs=pl.BlockSpec(memory_space=pltpu.VMEM),
    )(plan, inputs, cotangent)


def gradient_kernel(left_ref, rows_ref, out_ref, held_ref, sems):
    tile = left_ref.shape[0] // TILES
    copies = []
    for i in range(TILES):
        block = pl.ds(i * tile, tile)
        held_ref[block, :] = jnp.dot(
            left_ref[block, :], rows_ref[...], preferred_element_type=jnp.float32
        ).astype(held_ref.dtype)
        copies.append(pltpu.make_async_copy(held_ref.at[block], out_ref.at[block], sems.at[i]))
        copies[-1].start()
    for copy in copies:
        copy.wait()


def gradient(left, rows):
    units = left.shape[0]
    width = rows.shape[1]
    return pl.pallas_call(
        gradient_kernel,
        out_shape=jax.ShapeDtypeStruct((units, width), left.dtype),
        in_specs=[pl.BlockSpec(memory_space=pltpu.VMEM), pl.BlockSpec(memory_space=pltpu.VMEM)],
        out_specs=pl.BlockSpec(memory_space=pl.ANY),
        scratch_shapes=[pltpu.VMEM((units, width), left.dtype), pltpu.SemaphoreType.DMA((TILES,))],
        compiler_params=pltpu.CompilerParams(vmem_limit_bytes=8 << 20),
    )(left, rows)


def local(inputs, cotangent, plan, weights):
    hidden_units, width = weights.shape[1:]
    sections = lax.axis_size(SECTION)
    depth = lax.axis_size("zl")
    owners = lax.axis_size(OWNERS)
    core = lax.axis_index("core")
    twin = [(0, 1), (1, 0)]

    order = [
        first + (z + depth // 2) % depth
        for first in (*range(sections // 2, sections, depth), *range(0, sections // 2, depth))
        for z in range(depth)
    ]
    owner_order = [half * (owners // 2) + x for x in reversed(range(owners // 2)) for half in (1, 0)]
    rows = lax.all_to_all(
        pack(plan, inputs, cotangent, sections), SECTION, 0, 0, axis_index_groups=[order]
    ).reshape(-1, width)
    row_count = rows.shape[0]

    piece = weights.reshape(2, hidden_units // 2, width)
    piece_own, piece_sent = lax.optimization_barrier(
        (
            lax.dynamic_index_in_dim(piece, core, 0, keepdims=False),
            lax.dynamic_index_in_dim(piece, 1 - core, 0, keepdims=False),
        )
    )
    piece_twin = lax.ppermute(piece_sent, "core", twin)
    both_rows = lax.all_gather(rows, "core")
    rows_twin = lax.optimization_barrier(jnp.where(core == 0, both_rows[1], both_rows[0]))

    def project(values, matrix):
        return jnp.einsum("fd,rd->fr", matrix, values, preferred_element_type=jnp.float32)

    pieces = lax.optimization_barrier(jnp.concatenate([piece_own, piece_twin], axis=1))
    partial = project(jnp.concatenate([rows, rows_twin], axis=1), pieces)
    partial = partial.astype(jnp.bfloat16).reshape(owners, -1, row_count)
    gathered = lax.all_to_all(partial, OWNERS, 0, 0, axis_index_groups=[owner_order])
    gathered = gathered.reshape((owners // 2, 2) + gathered.shape[1:])
    near = jnp.sum(gathered.astype(jnp.float32), axis=0).astype(jnp.bfloat16)
    both = lax.all_gather(near, "zh")
    total = both[0].astype(jnp.float32) + both[1].astype(jnp.float32)
    pre_sum = total[1]
    grad_hidden = total[0].astype(jnp.bfloat16).astype(jnp.float32)
    logistic = jax.nn.sigmoid(pre_sum)
    hidden = (pre_sum * logistic).astype(jnp.bfloat16)
    grad_pre = (grad_hidden * logistic * (1.0 + pre_sum * (1.0 - logistic))).astype(jnp.bfloat16)

    answer = jnp.stack([hidden, grad_pre])
    answer = jnp.broadcast_to(answer[None], (owners // 2,) + answer.shape)
    answer = answer.reshape((owners,) + hidden.shape)
    left = lax.all_to_all(answer, OWNERS, 0, 0, axis_index_groups=[owner_order]).reshape(-1, row_count)
    whole = lax.all_gather(left, "core", axis=0, tiled=True)
    grads = gradient(whole, rows)
    return grads.reshape(1, hidden_units, width)


def solution(mesh):
    fine = Mesh(
        np.asarray(mesh.devices).reshape(2, 2, 8, 2, 4, 2),
        ("half", "yl", "zl", "zh", "x", "core"),
    )
    placed = (
        P(None, SECTION, TENSOR),
        P(None, SECTION, TENSOR),
        P(),
        P(SECTION, None, TENSOR),
    )
    return jax.shard_map(
        local, mesh=fine, in_specs=placed, out_specs=P(SECTION, None, TENSOR), check_vma=False
    )
```
